32 devices in a mesh: member: 2 (over x), patch: 16 (over z, y, core).
Axes of the slice: x: 2, y: 2, z: 4, core: 2. Of those that a mesh axis runs over, the one named last changes fastest.
Arguments:
- log_rate: float32 [65536, 128], P(('member', 'patch')), parts along dimension 0, may hold values from -3 to 3
- log_state: float32 [65536, 128], P(('member', 'patch')), parts along dimension 0, may hold values from -3 to 3
- near_blocks: bfloat16 [512, 12, 128, 128], P(('member', 'patch')), parts along dimension 0, may hold values from -0.15625 to 0.15625
- near_columns: int32 [512, 12], P(('member', 'patch')), parts along dimension 0, may hold values from 0 to 255, as said below
- far_basis: bfloat16 [8, 32, 32768], P('member', None, 'patch'), parts along dimension 0, may hold values from -0.0625 to 0.0625
- far_coupling: bfloat16 [8, 32, 32768], P('member', None, 'patch'), parts along dimension 0, may hold values from -0.5 to 0.5
- self_stiffness: float32 [65536], P(('member', 'patch')), parts along dimension 0, may hold values from 1 to 3
- plate_rate: float32 [65536], P(('member', 'patch')), parts along dimension 0, may hold values from 0.5 to 2
- direct_effect: float32 [65536], P(('member', 'patch')), parts along dimension 0, may hold values from 0.3 to 1
- evolution_effect: float32 [65536], P(('member', 'patch')), parts along dimension 0, may hold values from 0.5 to 1.5
- triangle_area: float32 [65536], P(('member', 'patch')), parts along dimension 0, may hold values from 0.5 to 10.5
Outputs:
- new_log_rate: float32 [65536, 128], P(('member', 'patch')), parts along dimension 0
- new_log_state: float32 [65536, 128], P(('member', 'patch')), parts along dimension 0
- error_norm: float32 [256], P('member'), parts along dimension 0
The draws below stay inside these ranges and needn't reach their ends.
There are 2 independent parts, one for each index of `member`. The reference program is written for one: setup_inputs(seed, part) draws one part's arguments, and reference() takes and returns one part's arrays. A program takes and returns all parts, laid end to end along the dimension named above; each array names one. Nothing has to cross between parts.
Inputs may be any that keep to these rules, and one draw needn't show every extreme that they name: `near_columns`: row block r's 12 column blocks are distinct, each is (r + o) mod 256 with -6 <= o <= 6, and they include r itself and both blocks at distance 6.
All inputs are finite; a program needn't handle non-finite values.
Results may differ from the reference program's by a relative error of at most 0.0012.
Values may be sent and summed in bfloat16 or wider, within the bound.
A program may use at most 128 MiB of HBM per device.

```python
import math
import jax
import jax.numpy as jnp
from jax import lax

BS = 128
R = 32
REACH = 6
NEAR = 12
SCEN = 128
NE_DEV = 2048
NBLK = 256
NE = 32768
LEVELS = 4
N_PATCH = 16


def draw_near_columns(key, part):
    spare_count = 2 * REACH - 2
    row_index = jnp.arange(NBLK, dtype=jnp.int32)
    key_pick, key_order = jax.random.split(key)
    candidates = jnp.concatenate([jnp.arange(-REACH + 1, 0, dtype=jnp.int32), jnp.arange(1, REACH, dtype=jnp.int32)])
    scores = jax.random.randint(key_pick, (NBLK, spare_count), 0, 1048576, dtype=jnp.int32) * spare_count + jnp.arange(spare_count, dtype=jnp.int32)[None, :]
    picked = jnp.take(candidates, jnp.argsort(scores, axis=1)[:, :NEAR - 3])
    fixed_part = jnp.broadcast_to(jnp.array([0, -REACH, REACH], dtype=jnp.int32), (NBLK, 3))
    offsets = jnp.concatenate([fixed_part, picked], axis=1)
    order_scores = jax.random.randint(key_order, (NBLK, NEAR), 0, 1048576, dtype=jnp.int32) * NEAR + jnp.arange(NEAR, dtype=jnp.int32)[None, :]
    offsets = jnp.take_along_axis(offsets, jnp.argsort(order_scores, axis=1), axis=1)
    return ((row_index[:, None] + offsets) % NBLK).astype(jnp.int32)


def draw_triangle_area(key, part):
    along = jnp.arange(NE, dtype=jnp.float32) / (NE - 1)
    rough = jnp.exp(jax.random.uniform(key, (NE,), jnp.float32, -0.35, 0.35))
    return (1.0 + 2.0 * along) * rough


def level_of(key, shape, pieces, low, high):
    level = 1.0
    for dim, shards_of in pieces:
        steps = jax.random.uniform(jax.random.fold_in(jax.random.fold_in(key, 6), dim), (shards_of,), jnp.float32, low / len(pieces), high / len(pieces))
        level = level * jnp.repeat(jnp.exp(steps), shape[dim] // shards_of).reshape((-1,) + (1,) * (len(shape) - 1 - dim))
    return level


def scatter_about(own_key, shape, scale, limit, pieces=(), kind=jnp.bfloat16):
    entries = scale * jax.random.normal(own_key, shape, jnp.float32)
    if pieces:
        entries = entries * level_of(own_key, shape, pieces, -0.22, 0.18)
    return jnp.clip(entries, -limit, limit).astype(kind)


def setup_inputs(seed: int = 0, part: int = 0) -> dict:
    splits = jax.random.split(jax.random.key(seed), 12)
    own_keys = jax.random.split(jax.random.fold_in(splits[11], part), 12)
    log_rate = scatter_about(own_keys[0], (NE, SCEN), 0.7, 3.0, ((0, 16),), jnp.float32)
    log_state = scatter_about(own_keys[1], (NE, SCEN), 0.7, 3.0, ((0, 16),), jnp.float32)
    near_blocks = scatter_about(own_keys[2], (NBLK, NEAR, BS, BS), (NEAR * BS) ** -0.5, 0.15625, ((0, 16),))
    near_columns = draw_near_columns(jax.random.fold_in(jax.random.fold_in(splits[11], part), 71), part)
    far_basis = scatter_about(own_keys[4], (LEVELS, R, NE), (4 * NE_DEV) ** -0.5, 0.0625, ((2, 16),))
    far_coupling = scatter_about(own_keys[5], (LEVELS, R, NE), (R * LEVELS) ** -0.5, 0.5, ((2, 16),))
    self_stiffness = jnp.clip(jnp.exp(math.log(3.0) - 1.0986123 * jax.random.uniform(own_keys[6], (NE,), jnp.float32) ** level_of(own_keys[6], (NE,), ((0, 16),), -0.2, 0.2)), 1.0, 3.0)
    plate_rate = jnp.clip(jnp.exp(math.log(2.0) - 1.3862944 * jax.random.uniform(own_keys[7], (NE,), jnp.float32) ** level_of(own_keys[7], (NE,), ((0, 16),), -0.2, 0.2)), 0.5, 2.0)
    direct_effect = jnp.clip(jnp.exp(math.log(1.0) - 1.2039728 * jax.random.uniform(own_keys[8], (NE,), jnp.float32) ** level_of(own_keys[8], (NE,), ((0, 16),), -0.2, 0.2)), 0.3, 1.0)
    evolution_effect = jnp.clip(jnp.exp(math.log(1.5) - 1.0986123 * jax.random.uniform(own_keys[9], (NE,), jnp.float32) ** level_of(own_keys[9], (NE,), ((0, 16),), -0.2, 0.2)), 0.5, 1.5)
    triangle_area = draw_triangle_area(jax.random.fold_in(jax.random.fold_in(splits[11], part), 71), part)
    return dict(log_rate=log_rate, log_state=log_state, near_blocks=near_blocks, near_columns=near_columns, far_basis=far_basis, far_coupling=far_coupling, self_stiffness=self_stiffness, plate_rate=plate_rate, direct_effect=direct_effect, evolution_effect=evolution_effect, triangle_area=triangle_area)


step_size = 0.1
damping = 0.5
error_scale = 0.01

def near_stress(rate_bf, near_blocks, near_columns):
    column_blocks = rate_bf.reshape(NBLK, BS, SCEN)

    def one_block(block_item):
        blocks, columns = block_item
        chosen = column_blocks[columns.astype(jnp.int32)]
        return jnp.einsum('kij,kjb->ib', blocks.astype(jnp.float32), chosen.astype(jnp.float32))
    result_rows = lax.map(one_block, (near_blocks, near_columns))
    return result_rows.reshape(NE, SCEN)

def far_stress(rate_bf, far_basis, far_coupling):
    leaves = rate_bf.reshape(N_PATCH, NE_DEV, SCEN).astype(jnp.float32)
    basis_four = far_basis.reshape(LEVELS, R, N_PATCH, NE_DEV).astype(jnp.float32)
    projected = jnp.einsum('lkci,cib->lckb', basis_four, leaves)
    coupled = []
    for tree_level in range(LEVELS):
        group_span = 2 ** tree_level
        group_sums = projected[tree_level].reshape(N_PATCH // (2 * group_span), 2, group_span, R, SCEN).sum(axis=2)
        sibling = group_sums[:, ::-1].reshape(N_PATCH // group_span, R, SCEN)
        coupled.append(jnp.repeat(sibling, group_span, axis=0))
    coupled = lax.optimization_barrier(jnp.stack(coupled).astype(jnp.bfloat16))
    coupling = far_coupling.reshape(LEVELS, R, N_PATCH, NE_DEV).astype(jnp.float32)
    result_rows = jnp.einsum('lkci,lckb->cib', coupling, coupled.astype(jnp.float32))
    return result_rows.reshape(NE, SCEN)

def section_rates(log_rate, log_state, near_blocks, near_columns, far_basis, far_coupling, self_stiffness, plate_rate, direct_effect, evolution_effect):
    velocity = jnp.exp(log_rate)
    rate_bf = lax.optimization_barrier(velocity.astype(jnp.bfloat16))
    near_term = near_stress(rate_bf, near_blocks, near_columns)
    far_term = far_stress(rate_bf, far_basis, far_coupling)
    stress_rate = self_stiffness[:, None] * (plate_rate[:, None] - velocity) - near_term - far_term
    state_rate = jnp.exp(-log_state) - velocity
    log_rate_rate = (stress_rate - evolution_effect[:, None] * state_rate) / (direct_effect[:, None] + damping * velocity)
    return (log_rate_rate, state_rate)

def reference(log_rate, log_state, near_blocks, near_columns, far_basis, far_coupling, self_stiffness, plate_rate, direct_effect, evolution_effect, triangle_area):
    fixed_args = (near_blocks, near_columns, far_basis, far_coupling, self_stiffness, plate_rate, direct_effect, evolution_effect)
    rate_one, state_one = section_rates(log_rate, log_state, *fixed_args)
    rate_two, state_two = section_rates(log_rate + step_size * rate_one, log_state + step_size * state_one, *fixed_args)
    half_step = 0.5 * step_size
    new_log_rate = log_rate + half_step * (rate_one + rate_two)
    new_log_state = log_state + half_step * (state_one + state_two)
    rate_error = half_step * (rate_two - rate_one) / error_scale
    state_error = half_step * (state_two - state_one) / error_scale
    totals = lax.optimization_barrier(jnp.sum(triangle_area[:, None] * (rate_error * rate_error + state_error * state_error), axis=0))
    area_total = jnp.sum(triangle_area)
    error_norm = jnp.sqrt(totals / area_total + 1e-06)
    return (new_log_rate, new_log_state, error_norm)
```

```python
import functools

import jax
import jax.numpy as jnp
from jax import lax
from jax.experimental import pallas as pl
from jax.experimental.pallas import tpu as pltpu
from jax.sharding import PartitionSpec as P

REACH = 6
WIDE = 2 * REACH + 1
GROUP = 4
PIECES = 4
HALF = REACH // 2

step_size = 0.1
damping = 0.5
error_scale = 0.01
MESH = pl.DeviceIdType.MESH


def flipped(me, mask):
    other = me
    bit = 1
    while bit <= mask:
        if mask & bit:
            other = other + bit * (1 - 2 * ((me // bit) % 2))
        bit *= 2
    return other


def kernel(
    n,
    rows,
    size,
    levels,
    rank,
    index_ref,
    log_rate,
    log_state,
    near,
    basis,
    coupling,
    stiff_in,
    plate_in,
    direct_in,
    evolve_in,
    area_in,
    rate_out,
    state_out,
    error_out,
    *scratch,
):
    near_bufs = scratch[:PIECES]
    (
        p_buf,
        s_buf,
        basis_buf,
        coupling_buf,
        coupling_t,
        vectors,
        columns,
        v_buf,
        kp_buf,
        ks_buf,
        acc,
        ext,
        send_a,
        recv_a,
        send_b,
        recv_b,
        err_send,
        err_recv,
        p_res,
        s_res,
        in_sems,
        near_sems,
        out_sems,
        halo_send,
        halo_recv,
        a_send,
        a_recv,
        b_send,
        b_recv,
        e_send,
        e_recv,
    ) = scratch[PIECES:]
    me = lax.axis_index("patch")
    right = lax.rem(me + 1, n)
    left = lax.rem(me + n - 1, n)
    per_piece = rows // PIECES
    near_count = near.shape[0] // rows
    groups = n // GROUP

    barrier = pltpu.get_barrier_semaphore()
    for mask in range(1, n):
        pl.semaphore_signal(
            barrier, inc=1, device_id={"patch": flipped(me, mask)}, device_id_type=MESH
        )

    def span(first, count=1):
        return pl.ds(first * size, count * size)

    loads = [
        pltpu.make_async_copy(log_rate, p_buf, in_sems.at[0]),
        pltpu.make_async_copy(basis, basis_buf, in_sems.at[1]),
        pltpu.make_async_copy(coupling, coupling_buf, in_sems.at[2]),
        pltpu.make_async_copy(log_state, s_buf, in_sems.at[3]),
    ]
    vector_loads = [
        pltpu.make_async_copy(source, vectors.at[pl.ds(i * rows, rows)], in_sems.at[4 + i])
        for i, source in enumerate((stiff_in, plate_in, direct_in, evolve_in, area_in))
    ]
    near_loads = [
        pltpu.make_async_copy(
            near.at[pl.ds(q * per_piece * near_count, per_piece * near_count)],
            near_bufs[q].at[pl.ds(0, per_piece * near_count)],
            near_sems.at[q],
        )
        for q in range(PIECES)
    ]
    loads[0].start()
    loads[1].start()
    for load in vector_loads:
        load.start()
    loads[2].start()
    for load in near_loads:
        load.start()
    loads[3].start()
    used = 5 * rows
    if vectors.shape[0] > used:
        vectors[used:, :] = jnp.zeros((vectors.shape[0] - used, size), jnp.float32)
    for q in range(PIECES):
        near_bufs[q][per_piece * near_count] = jnp.zeros((size, size), jnp.bfloat16)

    def halo_copy(section, way, piece):
        if way == 0:
            first, target, peer = HALF * piece, rows + REACH + HALF * piece, left
        else:
            first = rows - HALF * (piece + 1)
            target, peer = REACH - HALF * (piece + 1), right
        return pltpu.make_async_remote_copy(
            src_ref=ext.at[section, span(REACH + first, HALF)],
            dst_ref=ext.at[section, span(target, HALF)],
            send_sem=halo_send.at[section, way, piece],
            recv_sem=halo_recv.at[section, way, piece],
            device_id={"patch": peer},
            device_id_type=MESH,
        )

    def a_copy(section, mask):
        first = 0 if mask == 1 else rank
        part = pl.ds(first, levels * rank - first)
        return pltpu.make_async_remote_copy(
            src_ref=send_a.at[section, part],
            dst_ref=recv_a.at[section, mask - 1, part],
            send_sem=a_send.at[section, mask - 1],
            recv_sem=a_recv.at[section, mask - 1],
            device_id={"patch": flipped(me, mask)},
            device_id_type=MESH,
        )

    def b_copy(section, mask):
        level = mask.bit_length() + 1
        return pltpu.make_async_remote_copy(
            src_ref=send_b.at[section, pl.ds((level - 2) * rank, rank)],
            dst_ref=recv_b.at[section, mask - 1],
            send_sem=b_send.at[section, mask - 1],
            recv_sem=b_recv.at[section, mask - 1],
            device_id={"patch": flipped(me, mask * GROUP)},
            device_id_type=MESH,
        )

    def error_copy(mask):
        return pltpu.make_async_remote_copy(
            src_ref=err_send,
            dst_ref=err_recv.at[mask - 1],
            send_sem=e_send.at[mask - 1],
            recv_sem=e_recv.at[mask - 1],
            device_id={"patch": flipped(me, mask)},
            device_id_type=MESH,
        )

    def near_lhs(r, first, last):
        buf = near_bufs[r // per_piece]
        return [buf[index_ref[r * WIDE + o]] for o in range(first, last)]

    def column(vector, r):
        j = vector * rows + r
        return columns[:, j : j + 1]

    def project(section):
        projected = jnp.dot(
            basis_buf[...], ext[section, span(REACH, rows)], preferred_element_type=jnp.float32
        )
        send_a[section] = projected.astype(jnp.bfloat16)
        for mask in range(1, GROUP):
            a_copy(section, mask).start()
        return projected

    def local_near(section, some_rows):
        for r in some_rows:
            if section == 0 and r % per_piece == 0:
                near_loads[r // per_piece].wait()
            first = max(0, REACH - r)
            last = min(WIDE, rows + REACH - r)
            acc[span(r)] = jnp.dot(
                jnp.concatenate(near_lhs(r, first, last), axis=1),
                ext[section, span(r + first, last - first)],
                preferred_element_type=jnp.float32,
            )

    def exchange_groups(section, projected):
        for mask in range(1, GROUP):
            a_copy(section, mask).wait_recv()
        if groups > 1:
            total = projected[2 * rank :]
            for mask in range(1, GROUP):
                total = total + recv_a[section, mask - 1, pl.ds(2 * rank, (levels - 2) * rank)].astype(
                    jnp.float32
                )
            send_b[section] = total.astype(jnp.bfloat16)
            for mask in range(1, groups):
                b_copy(section, mask).start()

    def sibling_sums(section):
        parts = [recv_a[section, 0, pl.ds(0, rank)]]
        parts.append(
            (
                recv_a[section, 1, pl.ds(rank, rank)].astype(jnp.float32)
                + recv_a[section, 2, pl.ds(rank, rank)].astype(jnp.float32)
            ).astype(jnp.bfloat16)
        )
        for mask in range(1, groups):
            b_copy(section, mask).wait_recv()
        for level in range(2, levels):
            low = 2 ** (level - 2)
            total = recv_b[section, low - 1].astype(jnp.float32)
            for mask in range(low + 1, 2 * low):
                total = total + recv_b[section, mask - 1].astype(jnp.float32)
            parts.append(total.astype(jnp.bfloat16))
        return jnp.concatenate(parts, axis=0)

    def rates(section, r, coupled, state):
        lhs, rhs = [], []
        low, high = max(0, REACH - r), min(WIDE, rows + REACH - r)
        if low > 0:
            lhs += near_lhs(r, 0, low)
            rhs.append(ext[section, span(r, low)])
        if high < WIDE:
            lhs += near_lhs(r, high, WIDE)
            rhs.append(ext[section, span(r + high, WIDE - high)])
        lhs.append(coupling_t[span(r)])
        rhs.append(coupled)
        if len(rhs) > 1:
            lhs, rhs = jnp.concatenate(lhs, axis=1), jnp.concatenate(rhs, axis=0)
        else:
            lhs, rhs = lhs[0], rhs[0]
        stress = acc[span(r)] + jnp.dot(lhs, rhs, preferred_element_type=jnp.float32)
        velocity = v_buf[span(r)]
        state_rate = jnp.exp(-state) - velocity
        stress_rate = column(0, r) * (column(1, r) - velocity) - stress
        rate = (stress_rate - column(3, r) * state_rate) / (column(2, r) + damping * velocity)
        return rate, state_rate

    edge_order = (
        list(range(HALF))
        + list(range(rows - HALF, rows))
        + list(range(HALF, REACH))
        + list(range(rows - REACH, rows - HALF))
    )
    order = edge_order + list(range(REACH, rows - REACH))
    sends_after = {
        HALF - 1: [(0, 0)],
        rows - 1: [(1, 0)],
        REACH - 1: [(0, 1)],
        rows - HALF - 1: [(1, 1)],
    }

    loads[0].wait()

    def first_velocity(first, count):
        velocity = jnp.exp(p_buf[span(first, count)])
        v_buf[span(first, count)] = velocity
        ext[0, span(REACH + first, count)] = velocity.astype(jnp.bfloat16)

    first_velocity(0, REACH)
    first_velocity(rows - REACH, REACH)
    pl.semaphore_wait(barrier, n - 1)
    for piece in range(2):
        for way in range(2):
            halo_copy(0, way, piece).start()
    first_velocity(REACH, rows - 2 * REACH)
    loads[1].wait()
    projected = project(0)

    for load in vector_loads:
        load.wait()
    columns[...] = vectors[...].T
    loads[2].wait()
    for r in range(rows):
        coupling_t[span(r)] = coupling_buf[:, r * size : (r + 1) * size].T
    half_rows = rows // 2
    local_near(0, range(half_rows))
    exchange_groups(0, projected)
    local_near(0, range(half_rows, rows))
    loads[3].wait()
    for piece in range(2):
        for way in range(2):
            halo_copy(0, way, piece).wait_recv()
    coupled = sibling_sums(0)
    for r in order:
        state = s_buf[span(r)]
        rate, state_rate = rates(0, r, coupled, state)
        kp_buf[span(r)] = rate
        ks_buf[span(r)] = state_rate
        velocity = jnp.exp(p_buf[span(r)] + step_size * rate)
        v_buf[span(r)] = velocity
        ext[1, span(REACH + r)] = velocity.astype(jnp.bfloat16)
        for way, piece in sends_after.get(r, ()):
            halo_copy(1, way, piece).start()

    projected = project(1)
    local_near(1, range(half_rows))
    exchange_groups(1, projected)
    local_near(1, range(half_rows, rows))
    for piece in range(2):
        for way in range(2):
            halo_copy(1, way, piece).wait_recv()
    coupled = sibling_sums(1)
    half_step = 0.5 * step_size
    scale = half_step / error_scale
    weighted = jnp.zeros((8, v_buf.shape[1]), jnp.float32)
    results = []
    for r in order:
        state_one = ks_buf[span(r)]
        rate_one = kp_buf[span(r)]
        state = s_buf[span(r)]
        rate, state_rate = rates(1, r, coupled, state + step_size * state_one)
        p_res[span(r)] = p_buf[span(r)] + half_step * (rate_one + rate)
        s_res[span(r)] = state + half_step * (state_one + state_rate)
        for i, (source, target) in enumerate(((p_res, rate_out), (s_res, state_out))):
            store = pltpu.make_async_copy(
                source.at[span(r)], target.at[span(r)], out_sems.at[i, r]
            )
            store.start()
            results.append(store)
        rate_error = scale * (rate - rate_one)
        state_error = scale * (state_rate - state_one)
        squares = column(4, r) * (rate_error * rate_error + state_error * state_error)
        weighted = weighted + jnp.sum(squares.reshape(-1, 8, squares.shape[1]), axis=0)

    area = jnp.sum(vectors[4 * rows : 5 * rows, :])
    err_send[0:1, :] = jnp.sum(weighted, axis=0, keepdims=True)
    err_send[1:2, :] = jnp.full((1, weighted.shape[1]), area, jnp.float32)
    err_send[2:8, :] = jnp.zeros((6, weighted.shape[1]), jnp.float32)
    for mask in range(1, n):
        error_copy(mask).start()
    for section in range(2):
        for piece in range(2):
            for way in range(2):
                halo_copy(section, way, piece).wait_send()
        for mask in range(1, GROUP):
            a_copy(section, mask).wait_send()
        for mask in range(1, groups):
            b_copy(section, mask).wait_send()
    for mask in range(1, n):
        error_copy(mask).wait_recv()
    both = err_send[...]
    for mask in range(1, n):
        both = both + err_recv[mask - 1]
    error_out[...] = jnp.sqrt(both[0:1] / both[1:2] + 1e-06)
    for mask in range(1, n):
        error_copy(mask).wait_send()
    for store in results:
        store.wait()


def on_device(
    log_rate,
    log_state,
    near_blocks,
    near_columns,
    far_basis,
    far_coupling,
    self_stiffness,
    plate_rate,
    direct_effect,
    evolution_effect,
    triangle_area,
):
    row_count, scenarios = log_rate.shape
    rows, near_count, size, _ = near_blocks.shape
    n = lax.axis_size("patch")
    levels, rank, _ = far_basis.shape
    total_blocks = n * rows
    first_block = lax.axis_index("patch") * rows
    local_index = jnp.arange(rows, dtype=jnp.int32)
    per_piece = rows // PIECES
    slot = (near_columns - (first_block + local_index)[:, None] + total_blocks + REACH) % total_blocks
    hit = slot[:, None, :] == jnp.arange(WIDE, dtype=jnp.int32)[None, :, None]
    none = per_piece * near_count
    place = (local_index % per_piece)[:, None, None] * near_count + jnp.arange(
        near_count, dtype=jnp.int32
    )
    index = none + jnp.sum(jnp.where(hit, place - none, 0), axis=2)

    def by_block(vector):
        return vector.reshape(rows, size)

    padded_vectors = -(-5 * rows // 128) * 128
    far_rows = levels * rank
    groups = n // GROUP
    ext_rows = (rows + 2 * REACH) * size
    f32, bf16 = jnp.float32, jnp.bfloat16
    dma = pltpu.SemaphoreType.DMA
    anywhere = pl.BlockSpec(memory_space=pl.ANY)
    new_rate, new_state, error = pl.pallas_call(
        functools.partial(kernel, n, rows, size, levels, rank),
        out_shape=(
            jax.ShapeDtypeStruct((row_count, scenarios), f32),
            jax.ShapeDtypeStruct((row_count, scenarios), f32),
            jax.ShapeDtypeStruct((1, scenarios), f32),
        ),
        in_specs=[pl.BlockSpec(memory_space=pltpu.SMEM)] + [anywhere] * 10,
        out_specs=(anywhere, anywhere, pl.BlockSpec(memory_space=pltpu.VMEM)),
        scratch_shapes=[
            pltpu.VMEM((per_piece * near_count + 1, size, size), bf16) for _ in range(PIECES)
        ]
        + [
            pltpu.VMEM((row_count, scenarios), f32),
            pltpu.VMEM((row_count, scenarios), f32),
            pltpu.VMEM((far_rows, row_count), bf16),
            pltpu.VMEM((far_rows, row_count), bf16),
            pltpu.VMEM((row_count, far_rows), bf16),
            pltpu.VMEM((padded_vectors, size), f32),
            pltpu.VMEM((size, padded_vectors), f32),
            pltpu.VMEM((row_count, scenarios), f32),
            pltpu.VMEM((row_count, scenarios), f32),
            pltpu.VMEM((row_count, scenarios), f32),
            pltpu.VMEM((row_count, scenarios), f32),
            pltpu.VMEM((2, ext_rows, scenarios), bf16),
            pltpu.VMEM((2, far_rows, scenarios), bf16),
            pltpu.VMEM((2, GROUP - 1, far_rows, scenarios), bf16),
            pltpu.VMEM((2, (levels - 2) * rank, scenarios), bf16),
            pltpu.VMEM((2, groups - 1, rank, scenarios), bf16),
            pltpu.VMEM((8, scenarios), f32),
            pltpu.VMEM((n - 1, 8, scenarios), f32),
            pltpu.VMEM((row_count, scenarios), f32),
            pltpu.VMEM((row_count, scenarios), f32),
            dma((9,)),
            dma((PIECES,)),
            dma((2, rows)),
            dma((2, 2, 2)),
            dma((2, 2, 2)),
            dma((2, GROUP - 1)),
            dma((2, GROUP - 1)),
            dma((2, groups - 1)),
            dma((2, groups - 1)),
            dma((n - 1,)),
            dma((n - 1,)),
        ],
        compiler_params=pltpu.CompilerParams(
            collective_id=0, has_side_effects=True, vmem_limit_bytes=48 * 1024 * 1024
        ),
    )(
        index.reshape(-1),
        log_rate,
        log_state,
        near_blocks.reshape(rows * near_count, size, size),
        far_basis.reshape(far_rows, row_count),
        far_coupling.reshape(far_rows, row_count),
        by_block(self_stiffness),
        by_block(plate_rate),
        by_block(direct_effect),
        by_block(evolution_effect),
        by_block(triangle_area),
    )
    return (new_rate, new_state, error.reshape(-1))


def solution(mesh):
    in_specs = (
        P(("member", "patch"), None),
        P(("member", "patch"), None),
        P(("member", "patch"), None, None, None),
        P(("member", "patch"), None),
        P("member", None, "patch"),
        P("member", None, "patch"),
        P(("member", "patch")),
        P(("member", "patch")),
        P(("member", "patch")),
        P(("member", "patch")),
        P(("member", "patch")),
    )
    out_specs = (P(("member", "patch"), None), P(("member", "patch"), None), P("member"))
    return jax.shard_map(
        on_device, mesh=mesh, in_specs=in_specs, out_specs=out_specs, check_vma=False
    )
```

```python
import functools

import jax
import jax.numpy as jnp
from jax import lax
from jax.experimental import pallas as pl
from jax.experimental.pallas import tpu as pltpu
from jax.sharding import PartitionSpec as P

REACH = 6
WIDE = 2 * REACH + 1
GROUP = 4
PIECES = 4
HALF = REACH // 2

step_size = 0.1
damping = 0.5
error_scale = 0.01
MESH = pl.DeviceIdType.MESH


def flipped(me, mask):
    other = me
    bit = 1
    while bit <= mask:
        if mask & bit:
            other = other + bit * (1 - 2 * ((me // bit) % 2))
        bit *= 2
    return other


def kernel(
    n,
    rows,
    size,
    levels,
    rank,
    index_ref,
    log_rate,
    log_state,
    near,
    basis,
    coupling,
    stiff_in,
    plate_in,
    direct_in,
    evolve_in,
    area_in,
    rate_out,
    state_out,
    error_out,
    *scratch,
):
    near_bufs = scratch[:PIECES]
    (
        p_buf,
        s_buf,
        basis_buf,
        coupling_buf,
        coupling_t,
        vectors,
        columns,
        v_buf,
        kp_buf,
        ks_buf,
        acc,
        ext,
        send_a,
        recv_a,
        send_b,
        recv_b,
        err_send,
        err_recv,
        p_res,
        s_res,
        in_sems,
        near_sems,
        out_sems,
        halo_send,
        halo_recv,
        a_send,
        a_recv,
        b_send,
        b_recv,
        e_send,
        e_recv,
    ) = scratch[PIECES:]
    me = lax.axis_index("patch")
    right = lax.rem(me + 1, n)
    left = lax.rem(me + n - 1, n)
    per_piece = rows // PIECES
    near_count = near.shape[0] // rows
    groups = n // GROUP

    barrier = pltpu.get_barrier_semaphore()
    for mask in range(1, n):
        pl.semaphore_signal(
            barrier, inc=1, device_id={"patch": flipped(me, mask)}, device_id_type=MESH
        )

    def span(first, count=1):
        return pl.ds(first * size, count * size)

    loads = [
        pltpu.make_async_copy(log_rate, p_buf, in_sems.at[0]),
        pltpu.make_async_copy(basis, basis_buf, in_sems.at[1]),
        pltpu.make_async_copy(coupling, coupling_buf, in_sems.at[2]),
        pltpu.make_async_copy(log_state, s_buf, in_sems.at[3]),
    ]
    vector_loads = [
        pltpu.make_async_copy(source, vectors.at[pl.ds(i * rows, rows)], in_sems.at[4 + i])
        for i, source in enumerate((stiff_in, plate_in, direct_in, evolve_in, area_in))
    ]
    near_loads = [
        pltpu.make_async_copy(
            near.at[pl.ds(q * per_piece * near_count, per_piece * near_count)],
            near_bufs[q].at[pl.ds(0, per_piece * near_count)],
            near_sems.at[q],
        )
        for q in range(PIECES)
    ]
    loads[0].start()
    loads[1].start()
    for load in vector_loads:
        load.start()
    loads[2].start()
    for load in near_loads:
        load.start()
    loads[3].start()
    used = 5 * rows
    if vectors.shape[0] > used:
        vectors[used:, :] = jnp.zeros((vectors.shape[0] - used, size), jnp.float32)
    for q in range(PIECES):
        near_bufs[q][per_piece * near_count] = jnp.zeros((size, size), jnp.bfloat16)

    def halo_copy(section, way, piece):
        if way == 0:
            first, target, peer = HALF * piece, rows + REACH + HALF * piece, left
        else:
            first = rows - HALF * (piece + 1)
            target, peer = REACH - HALF * (piece + 1), right
        return pltpu.make_async_remote_copy(
            src_ref=ext.at[section, span(REACH + first, HALF)],
            dst_ref=ext.at[section, span(target, HALF)],
            send_sem=halo_send.at[section, way, piece],
            recv_sem=halo_recv.at[section, way, piece],
            device_id={"patch": peer},
            device_id_type=MESH,
        )

    def a_copy(section, mask):
        first = 0 if mask == 1 else rank
        part = pl.ds(first, levels * rank - first)
        return pltpu.make_async_remote_copy(
            src_ref=send_a.at[section, part],
            dst_ref=recv_a.at[section, mask - 1, part],
            send_sem=a_send.at[section, mask - 1],
            recv_sem=a_recv.at[section, mask - 1],
            device_id={"patch": flipped(me, mask)},
            device_id_type=MESH,
        )

    def b_copy(section, mask):
        level = mask.bit_length() + 1
        return pltpu.make_async_remote_copy(
            src_ref=send_b.at[section, pl.ds((level - 2) * rank, rank)],
            dst_ref=recv_b.at[section, mask - 1],
            send_sem=b_send.at[section, mask - 1],
            recv_sem=b_recv.at[section, mask - 1],
            device_id={"patch": flipped(me, mask * GROUP)},
            device_id_type=MESH,
        )

    def error_copy(mask):
        return pltpu.make_async_remote_copy(
            src_ref=err_send,
            dst_ref=err_recv.at[mask - 1],
            send_sem=e_send.at[mask - 1],
            recv_sem=e_recv.at[mask - 1],
            device_id={"patch": flipped(me, mask)},
            device_id_type=MESH,
        )

    near_waits = [True] * PIECES

    def near_block(r, offset):
        buf = near_bufs[r // per_piece]
        if 0 <= offset < WIDE:
            return buf[index_ref[r * WIDE + offset]]
        return buf[per_piece * near_count]

    def column(vector, r):
        j = vector * rows + r
        return columns[:, j : j + 1]

    def project(section):
        projected = jnp.dot(
            basis_buf[...], ext[section, span(REACH, rows)], preferred_element_type=jnp.float32
        )
        send_a[section] = projected.astype(jnp.bfloat16)
        for mask in range(1, GROUP):
            a_copy(section, mask).start()
        return projected

    def near_pairs(section, pairs, fresh):
        for j in pairs:
            users = range(max(0, 2 * j - 2 * REACH), min(rows, 2 * j + 2))
            if section == 0:
                for q in range(PIECES):
                    if near_waits[q] and q * per_piece in users:
                        near_loads[q].wait()
                        near_waits[q] = False
            lhs = jnp.concatenate(
                [
                    jnp.concatenate([near_block(r, 2 * j - r), near_block(r, 2 * j + 1 - r)], axis=1)
                    for r in users
                ],
                axis=0,
            )
            product = jnp.dot(lhs, ext[section, span(2 * j, 2)], preferred_element_type=jnp.float32)
            for i, r in enumerate(users):
                part = product[i * size : (i + 1) * size]
                if r in fresh:
                    acc[span(r)] = part
                    fresh.discard(r)
                else:
                    acc[span(r)] += part

    def exchange_groups(section, projected):
        for mask in range(1, GROUP):
            a_copy(section, mask).wait_recv()
        if groups > 1:
            total = projected[2 * rank :]
            for mask in range(1, GROUP):
                total = total + recv_a[section, mask - 1, pl.ds(2 * rank, (levels - 2) * rank)].astype(
                    jnp.float32
                )
            send_b[section] = total.astype(jnp.bfloat16)
            for mask in range(1, groups):
                b_copy(section, mask).start()

    def sibling_sums(section):
        parts = [recv_a[section, 0, pl.ds(0, rank)]]
        parts.append(
            (
                recv_a[section, 1, pl.ds(rank, rank)].astype(jnp.float32)
                + recv_a[section, 2, pl.ds(rank, rank)].astype(jnp.float32)
            ).astype(jnp.bfloat16)
        )
        for mask in range(1, groups):
            b_copy(section, mask).wait_recv()
        for level in range(2, levels):
            low = 2 ** (level - 2)
            total = recv_b[section, low - 1].astype(jnp.float32)
            for mask in range(low + 1, 2 * low):
                total = total + recv_b[section, mask - 1].astype(jnp.float32)
            parts.append(total.astype(jnp.bfloat16))
        return jnp.concatenate(parts, axis=0)

    def rates(r, far, state):
        stress = acc[span(r)] + far
        velocity = v_buf[span(r)]
        state_rate = jnp.exp(-state) - velocity
        stress_rate = column(0, r) * (column(1, r) - velocity) - stress
        rate = (stress_rate - column(3, r) * state_rate) / (column(2, r) + damping * velocity)
        return rate, state_rate

    def far_rows_of(first, count, coupled):
        far = jnp.dot(coupling_t[span(first, count)], coupled, preferred_element_type=jnp.float32)
        return [(first + i, far[i * size : (i + 1) * size]) for i in range(count)]

    halo_pairs = HALF
    local_pairs = list(range(halo_pairs, halo_pairs + rows // 2))
    edge_pairs = list(range(halo_pairs)) + list(
        range(halo_pairs + rows // 2, 2 * halo_pairs + rows // 2)
    )
    early, late = local_pairs[: rows // 4], local_pairs[rows // 4 :]

    row_groups = [
        (0, HALF),
        (rows - HALF, HALF),
        (HALF, HALF),
        (rows - REACH, HALF),
        (REACH, rows - 2 * REACH),
    ]
    sends_after = {
        HALF - 1: [(0, 0)],
        rows - 1: [(1, 0)],
        REACH - 1: [(0, 1)],
        rows - HALF - 1: [(1, 1)],
    }

    loads[0].wait()

    def first_velocity(first, count):
        velocity = jnp.exp(p_buf[span(first, count)])
        v_buf[span(first, count)] = velocity
        ext[0, span(REACH + first, count)] = velocity.astype(jnp.bfloat16)

    first_velocity(0, REACH)
    first_velocity(rows - REACH, REACH)
    pl.semaphore_wait(barrier, n - 1)
    for piece in range(2):
        for way in range(2):
            halo_copy(0, way, piece).start()
    first_velocity(REACH, rows - 2 * REACH)
    loads[1].wait()
    projected = project(0)

    for load in vector_loads:
        load.wait()
    columns[...] = vectors[...].T
    loads[2].wait()
    for r in range(rows):
        coupling_t[span(r)] = coupling_buf[:, r * size : (r + 1) * size].T
    fresh = set(range(rows))
    near_pairs(0, early, fresh)
    exchange_groups(0, projected)
    near_pairs(0, late, fresh)
    loads[3].wait()
    for piece in range(2):
        for way in range(2):
            halo_copy(0, way, piece).wait_recv()
    near_pairs(0, edge_pairs, fresh)
    coupled = sibling_sums(0)
    for r, far in (item for first, count in row_groups for item in far_rows_of(first, count, coupled)):
        state = s_buf[span(r)]
        rate, state_rate = rates(r, far, state)
        kp_buf[span(r)] = rate
        ks_buf[span(r)] = state_rate
        velocity = jnp.exp(p_buf[span(r)] + step_size * rate)
        v_buf[span(r)] = velocity
        ext[1, span(REACH + r)] = velocity.astype(jnp.bfloat16)
        for way, piece in sends_after.get(r, ()):
            halo_copy(1, way, piece).start()

    projected = project(1)
    fresh = set(range(rows))
    near_pairs(1, early, fresh)
    exchange_groups(1, projected)
    near_pairs(1, late, fresh)
    for piece in range(2):
        for way in range(2):
            halo_copy(1, way, piece).wait_recv()
    near_pairs(1, edge_pairs, fresh)
    coupled = sibling_sums(1)
    half_step = 0.5 * step_size
    scale = half_step / error_scale
    weighted = jnp.zeros((8, v_buf.shape[1]), jnp.float32)
    results = []
    for r, far in (item for first, count in row_groups for item in far_rows_of(first, count, coupled)):
        state_one = ks_buf[span(r)]
        rate_one = kp_buf[span(r)]
        state = s_buf[span(r)]
        rate, state_rate = rates(r, far, state + step_size * state_one)
        p_res[span(r)] = p_buf[span(r)] + half_step * (rate_one + rate)
        s_res[span(r)] = state + half_step * (state_one + state_rate)
        for i, (source, target) in enumerate(((p_res, rate_out), (s_res, state_out))):
            store = pltpu.make_async_copy(
                source.at[span(r)], target.at[span(r)], out_sems.at[i, r]
            )
            store.start()
            results.append(store)
        rate_error = scale * (rate - rate_one)
        state_error = scale * (state_rate - state_one)
        squares = column(4, r) * (rate_error * rate_error + state_error * state_error)
        weighted = weighted + jnp.sum(squares.reshape(-1, 8, squares.shape[1]), axis=0)

    area = jnp.sum(vectors[4 * rows : 5 * rows, :])
    err_send[0:1, :] = jnp.sum(weighted, axis=0, keepdims=True)
    err_send[1:2, :] = jnp.full((1, weighted.shape[1]), area, jnp.float32)
    err_send[2:8, :] = jnp.zeros((6, weighted.shape[1]), jnp.float32)
    for mask in range(1, n):
        error_copy(mask).start()
    for section in range(2):
        for piece in range(2):
            for way in range(2):
                halo_copy(section, way, piece).wait_send()
        for mask in range(1, GROUP):
            a_copy(section, mask).wait_send()
        for mask in range(1, groups):
            b_copy(section, mask).wait_send()
    for mask in range(1, n):
        error_copy(mask).wait_recv()
    both = err_send[...]
    for mask in range(1, n):
        both = both + err_recv[mask - 1]
    error_out[...] = jnp.sqrt(both[0:1] / both[1:2] + 1e-06)
    for mask in range(1, n):
        error_copy(mask).wait_send()
    for store in results:
        store.wait()


def store_kernel(rate_in, state_in, error_in, rate_out, state_out, error_out, sems):
    part = rate_in.shape[0] // PIECES
    copies = [pltpu.make_async_copy(error_in, error_out, sems.at[2 * PIECES])]
    for i, (source, target) in enumerate(((rate_in, rate_out), (state_in, state_out))):
        for q in range(PIECES):
            piece = pl.ds(q * part, part)
            copies.append(
                pltpu.make_async_copy(
                    source.at[piece], target.at[piece], sems.at[i * PIECES + q]
                )
            )
    for copy in copies:
        copy.start()
    for copy in copies:
        copy.wait()


def on_device(
    log_rate,
    log_state,
    near_blocks,
    near_columns,
    far_basis,
    far_coupling,
    self_stiffness,
    plate_rate,
    direct_effect,
    evolution_effect,
    triangle_area,
):
    row_count, scenarios = log_rate.shape
    rows, near_count, size, _ = near_blocks.shape
    n = lax.axis_size("patch")
    levels, rank, _ = far_basis.shape
    total_blocks = n * rows
    first_block = lax.axis_index("patch") * rows
    local_index = jnp.arange(rows, dtype=jnp.int32)
    per_piece = rows // PIECES
    slot = (near_columns - (first_block + local_index)[:, None] + total_blocks + REACH) % total_blocks
    hit = slot[:, None, :] == jnp.arange(WIDE, dtype=jnp.int32)[None, :, None]
    none = per_piece * near_count
    place = (local_index % per_piece)[:, None, None] * near_count + jnp.arange(
        near_count, dtype=jnp.int32
    )
    index = none + jnp.sum(jnp.where(hit, place - none, 0), axis=2)

    def by_block(vector):
        return vector.reshape(rows, size)

    padded_vectors = -(-5 * rows // 128) * 128
    far_rows = levels * rank
    groups = n // GROUP
    ext_rows = (rows + 2 * REACH) * size
    f32, bf16 = jnp.float32, jnp.bfloat16
    dma = pltpu.SemaphoreType.DMA
    anywhere = pl.BlockSpec(memory_space=pl.ANY)
    in_hbm = pl.BlockSpec(memory_space=pltpu.HBM)
    new_rate, new_state, error = pl.pallas_call(
        functools.partial(kernel, n, rows, size, levels, rank),
        out_shape=(
            jax.ShapeDtypeStruct((row_count, scenarios), f32),
            jax.ShapeDtypeStruct((row_count, scenarios), f32),
            jax.ShapeDtypeStruct((1, scenarios), f32),
        ),
        in_specs=[pl.BlockSpec(memory_space=pltpu.SMEM)] + [in_hbm] * 10,
        out_specs=(anywhere, anywhere, pl.BlockSpec(memory_space=pltpu.VMEM)),
        scratch_shapes=[
            pltpu.VMEM((per_piece * near_count + 1, size, size), bf16) for _ in range(PIECES)
        ]
        + [
            pltpu.VMEM((row_count, scenarios), f32),
            pltpu.VMEM((row_count, scenarios), f32),
            pltpu.VMEM((far_rows, row_count), bf16),
            pltpu.VMEM((far_rows, row_count), bf16),
            pltpu.VMEM((row_count, far_rows), bf16),
            pltpu.VMEM((padded_vectors, size), f32),
            pltpu.VMEM((size, padded_vectors), f32),
            pltpu.VMEM((row_count, scenarios), f32),
            pltpu.VMEM((row_count, scenarios), f32),
            pltpu.VMEM((row_count, scenarios), f32),
            pltpu.VMEM((row_count, scenarios), f32),
            pltpu.VMEM((2, ext_rows, scenarios), bf16),
            pltpu.VMEM((2, far_rows, scenarios), bf16),
            pltpu.VMEM((2, GROUP - 1, far_rows, scenarios), bf16),
            pltpu.VMEM((2, (levels - 2) * rank, scenarios), bf16),
            pltpu.VMEM((2, groups - 1, rank, scenarios), bf16),
            pltpu.VMEM((8, scenarios), f32),
            pltpu.VMEM((n - 1, 8, scenarios), f32),
            pltpu.VMEM((row_count, scenarios), f32),
            pltpu.VMEM((row_count, scenarios), f32),
            dma((9,)),
            dma((PIECES,)),
            dma((2, rows)),
            dma((2, 2, 2)),
            dma((2, 2, 2)),
            dma((2, GROUP - 1)),
            dma((2, GROUP - 1)),
            dma((2, groups - 1)),
            dma((2, groups - 1)),
            dma((n - 1,)),
            dma((n - 1,)),
        ],
        compiler_params=pltpu.CompilerParams(
            collective_id=0, has_side_effects=True, vmem_limit_bytes=60 * 1024 * 1024
        ),
    )(
        index.reshape(-1),
        log_rate,
        log_state,
        near_blocks.reshape(rows * near_count, size, size),
        far_basis.reshape(far_rows, row_count),
        far_coupling.reshape(far_rows, row_count),
        by_block(self_stiffness),
        by_block(plate_rate),
        by_block(direct_effect),
        by_block(evolution_effect),
        by_block(triangle_area),
    )
    outputs = [
        jax.ShapeDtypeStruct((row_count, scenarios), f32),
        jax.ShapeDtypeStruct((row_count, scenarios), f32),
        jax.ShapeDtypeStruct((1, scenarios), f32),
    ]
    new_rate, new_state, error = pl.pallas_call(
        store_kernel,
        out_shape=outputs,
        in_specs=[anywhere] * 3,
        out_specs=[in_hbm] * 3,
        scratch_shapes=[dma((2 * PIECES + 1,))],
        compiler_params=pltpu.CompilerParams(vmem_limit_bytes=60 * 1024 * 1024),
    )(new_rate, new_state, error)
    return (new_rate, new_state, error.reshape(-1))


def solution(mesh):
    in_specs = (
        P(("member", "patch"), None),
        P(("member", "patch"), None),
        P(("member", "patch"), None, None, None),
        P(("member", "patch"), None),
        P("member", None, "patch"),
        P("member", None, "patch"),
        P(("member", "patch")),
        P(("member", "patch")),
        P(("member", "patch")),
        P(("member", "patch")),
        P(("member", "patch")),
    )
    out_specs = (P(("member", "patch"), None), P(("member", "patch"), None), P("member"))
    return jax.shard_map(
        on_device, mesh=mesh, in_specs=in_specs, out_specs=out_specs, check_vma=False
    )
```

```python
import functools

import jax
import jax.numpy as jnp
from jax import lax
from jax.experimental import pallas as pl
from jax.experimental.pallas import tpu as pltpu
from jax.sharding import PartitionSpec as P

REACH = 6
WIDE = 2 * REACH + 1
PIECES = 4
HALF = REACH // 2

step_size = 0.1
damping = 0.5
error_scale = 0.01
MESH = pl.DeviceIdType.MESH


def flipped(me, mask):
    other = me
    bit = 1
    while bit <= mask:
        if mask & bit:
            other = other + bit * (1 - 2 * ((me // bit) % 2))
        bit *= 2
    return other


def kernel(
    n,
    rows,
    size,
    levels,
    rank,
    index_ref,
    log_rate,
    log_state,
    near,
    basis,
    coupling,
    stiff_in,
    plate_in,
    direct_in,
    evolve_in,
    area_in,
    rate_out,
    state_out,
    error_out,
    *scratch,
):
    near_bufs = scratch[:PIECES]
    (
        p_buf,
        s_buf,
        basis_buf,
        coupling_buf,
        coupling_t,
        vectors,
        columns,
        v_buf,
        kp_buf,
        ks_buf,
        acc,
        ext,
        far_send,
        far_recv,
        err_send,
        err_recv,
        p_res,
        s_res,
        rate_sems,
        in_sems,
        near_sems,
        out_sems,
        halo_send,
        halo_recv,
        f_send,
        f_recv,
        e_send,
        e_recv,
    ) = scratch[PIECES:]
    me = lax.axis_index("patch")
    right = lax.rem(me + 1, n)
    left = lax.rem(me + n - 1, n)
    per_piece = rows // PIECES
    near_count = near.shape[0] // rows

    barrier = pltpu.get_barrier_semaphore()
    for mask in range(1, n):
        pl.semaphore_signal(
            barrier, inc=1, device_id={"patch": flipped(me, mask)}, device_id_type=MESH
        )

    def span(first, count=1):
        return pl.ds(first * size, count * size)

    quarter = [pl.ds(q * (rows // PIECES) * size, (rows // PIECES) * size) for q in range(PIECES)]
    rate_loads = [
        pltpu.make_async_copy(log_rate.at[part], p_buf.at[part], rate_sems.at[q])
        for q, part in enumerate(quarter)
    ]
    loads = [
        pltpu.make_async_copy(basis, basis_buf, in_sems.at[1]),
        pltpu.make_async_copy(coupling, coupling_buf, in_sems.at[2]),
        pltpu.make_async_copy(log_state, s_buf, in_sems.at[3]),
    ]
    vector_loads = [
        pltpu.make_async_copy(source, vectors.at[pl.ds(i * rows, rows)], in_sems.at[4 + i])
        for i, source in enumerate((stiff_in, plate_in, direct_in, evolve_in, area_in))
    ]
    near_loads = [
        pltpu.make_async_copy(
            near.at[pl.ds(q * per_piece * near_count, per_piece * near_count)],
            near_bufs[q].at[pl.ds(0, per_piece * near_count)],
            near_sems.at[q],
        )
        for q in range(PIECES)
    ]
    for load in rate_loads:
        load.start()
    loads[0].start()
    for load in vector_loads:
        load.start()
    loads[1].start()
    for load in near_loads:
        load.start()
    loads[2].start()
    used = 5 * rows
    if vectors.shape[0] > used:
        vectors[used:, :] = jnp.zeros((vectors.shape[0] - used, size), jnp.float32)
    for q in range(PIECES):
        near_bufs[q][per_piece * near_count] = jnp.zeros((size, size), jnp.bfloat16)

    def halo_copy(section, way, piece):
        if way == 0:
            first, target, peer = HALF * piece, rows + REACH + HALF * piece, left
        else:
            first = rows - HALF * (piece + 1)
            target, peer = REACH - HALF * (piece + 1), right
        return pltpu.make_async_remote_copy(
            src_ref=ext.at[section, span(REACH + first, HALF)],
            dst_ref=ext.at[section, span(target, HALF)],
            send_sem=halo_send.at[section, way, piece],
            recv_sem=halo_recv.at[section, way, piece],
            device_id={"patch": peer},
            device_id_type=MESH,
        )

    def far_copy(section, mask):
        level = mask.bit_length() - 1
        return pltpu.make_async_remote_copy(
            src_ref=far_send.at[section, pl.ds(level * rank, rank)],
            dst_ref=far_recv.at[section, mask - 1],
            send_sem=f_send.at[section, mask - 1],
            recv_sem=f_recv.at[section, mask - 1],
            device_id={"patch": flipped(me, mask)},
            device_id_type=MESH,
        )

    def error_copy(mask):
        return pltpu.make_async_remote_copy(
            src_ref=err_send,
            dst_ref=err_recv.at[mask - 1],
            send_sem=e_send.at[mask - 1],
            recv_sem=e_recv.at[mask - 1],
            device_id={"patch": flipped(me, mask)},
            device_id_type=MESH,
        )

    near_waits = [True] * PIECES

    def near_block(r, offset):
        buf = near_bufs[r // per_piece]
        if 0 <= offset < WIDE:
            return buf[index_ref[r, offset]]
        return buf[per_piece * near_count]

    def column(vector, r):
        return columns[vector, span(r)]

    def project(section):
        projected = jnp.dot(
            basis_buf[...], ext[section, span(REACH, rows)], preferred_element_type=jnp.float32
        )
        far_send[section] = projected.astype(jnp.bfloat16)
        for mask in range(1, n):
            far_copy(section, mask).start()

    def near_pairs(section, pairs, fresh):
        for j in pairs:
            users = range(max(0, 2 * j - 2 * REACH), min(rows, 2 * j + 2))
            if section == 0:
                for q in range(PIECES):
                    if near_waits[q] and q * per_piece in users:
                        near_loads[q].wait()
                        near_waits[q] = False
            lhs = jnp.concatenate(
                [
                    jnp.concatenate([near_block(r, 2 * j - r), near_block(r, 2 * j + 1 - r)], axis=1)
                    for r in users
                ],
                axis=0,
            )
            product = jnp.dot(lhs, ext[section, span(2 * j, 2)], preferred_element_type=jnp.float32)
            for i, r in enumerate(users):
                part = product[i * size : (i + 1) * size]
                if r in fresh:
                    acc[span(r)] = part
                    fresh.discard(r)
                else:
                    acc[span(r)] += part

    def sibling_sums(section):
        for mask in range(1, n):
            far_copy(section, mask).wait_recv()
        parts = []
        for level in range(levels):
            low = 2**level
            total = far_recv[section, low - 1].astype(jnp.float32)
            for mask in range(low + 1, 2 * low):
                total = total + far_recv[section, mask - 1].astype(jnp.float32)
            parts.append(total.astype(jnp.bfloat16))
        return jnp.concatenate(parts, axis=0)

    def rates(r, far, state):
        stress = acc[span(r)] + far
        velocity = v_buf[span(r)]
        state_rate = jnp.exp(-state) - velocity
        stress_rate = column(0, r) * (column(1, r) - velocity) - stress
        rate = (stress_rate - column(3, r) * state_rate) / (column(2, r) + damping * velocity)
        return rate, state_rate

    local_pairs = range(HALF, HALF + rows // 2)
    left_pairs = range(HALF)
    right_pairs = range(HALF + rows // 2, 2 * HALF + rows // 2)

    def finished_rows(section, fresh):
        coupled = None
        for way, pairs, parts in (
            (1, left_pairs, ((0, HALF), (HALF, HALF))),
            (0, right_pairs, ((rows - HALF, HALF), (rows - REACH, HALF))),
            (None, (), ((REACH, rows - 2 * REACH),)),
        ):
            if way is not None:
                for piece in range(2):
                    halo_copy(section, way, piece).wait_recv()
            near_pairs(section, pairs, fresh)
            if coupled is None:
                coupled = sibling_sums(section)
            for first, count in parts:
                far = jnp.dot(
                    coupling_t[span(first, count)], coupled, preferred_element_type=jnp.float32
                )
                for i in range(count):
                    yield first + i, far[i * size : (i + 1) * size]

    sends_after = {
        HALF - 1: [(0, 0)],
        rows - 1: [(1, 0)],
        REACH - 1: [(0, 1)],
        rows - HALF - 1: [(1, 1)],
    }

    for load in rate_loads:
        load.wait()

    def first_velocity(first, count):
        velocity = jnp.exp(p_buf[span(first, count)])
        v_buf[span(first, count)] = velocity
        ext[0, span(REACH + first, count)] = velocity.astype(jnp.bfloat16)

    first_velocity(0, REACH)
    first_velocity(rows - REACH, REACH)
    pl.semaphore_wait(barrier, n - 1)
    for piece in range(2):
        for way in range(2):
            halo_copy(0, way, piece).start()
    first_velocity(REACH, rows - 2 * REACH)
    loads[0].wait()
    project(0)

    for load in vector_loads:
        load.wait()
    turned = vectors[...].T
    for vector in range(5):
        for r in range(rows):
            j = vector * rows + r
            columns[vector, span(r)] = jnp.broadcast_to(
                turned[:, j : j + 1], (size, columns.shape[2])
            )
    loads[1].wait()
    for r in range(rows):
        coupling_t[span(r)] = coupling_buf[:, r * size : (r + 1) * size].T
    fresh = set(range(rows))
    near_pairs(0, local_pairs, fresh)
    loads[2].wait()
    for r, far in finished_rows(0, fresh):
        state = s_buf[span(r)]
        rate, state_rate = rates(r, far, state)
        kp_buf[span(r)] = rate
        ks_buf[span(r)] = state_rate
        velocity = jnp.exp(p_buf[span(r)] + step_size * rate)
        v_buf[span(r)] = velocity
        ext[1, span(REACH + r)] = velocity.astype(jnp.bfloat16)
        for way, piece in sends_after.get(r, ()):
            halo_copy(1, way, piece).start()

    project(1)
    fresh = set(range(rows))
    near_pairs(1, local_pairs, fresh)
    half_step = 0.5 * step_size
    scale = half_step / error_scale
    weighted = jnp.zeros((8, v_buf.shape[1]), jnp.float32)
    results = []
    for r, far in finished_rows(1, fresh):
        state_one = ks_buf[span(r)]
        rate_one = kp_buf[span(r)]
        state = s_buf[span(r)]
        rate, state_rate = rates(r, far, state + step_size * state_one)
        p_res[span(r)] = p_buf[span(r)] + half_step * (rate_one + rate)
        s_res[span(r)] = state + half_step * (state_one + state_rate)
        for i, (source, target) in enumerate(((p_res, rate_out), (s_res, state_out))):
            store = pltpu.make_async_copy(
                source.at[span(r)], target.at[span(r)], out_sems.at[i, r]
            )
            store.start()
            results.append(store)
        rate_error = scale * (rate - rate_one)
        state_error = scale * (state_rate - state_one)
        squares = column(4, r) * (rate_error * rate_error + state_error * state_error)
        weighted = weighted + jnp.sum(squares.reshape(-1, 8, squares.shape[1]), axis=0)

    area = jnp.sum(vectors[4 * rows : 5 * rows, :])
    err_send[0:1, :] = jnp.sum(weighted, axis=0, keepdims=True)
    err_send[1:2, :] = jnp.full((1, weighted.shape[1]), area, jnp.float32)
    err_send[2:8, :] = jnp.zeros((6, weighted.shape[1]), jnp.float32)
    for mask in range(1, n):
        error_copy(mask).start()
    for section in range(2):
        for piece in range(2):
            for way in range(2):
                halo_copy(section, way, piece).wait_send()
        for mask in range(1, n):
            far_copy(section, mask).wait_send()
    for mask in range(1, n):
        error_copy(mask).wait_recv()
    both = err_send[...]
    for mask in range(1, n):
        both = both + err_recv[mask - 1]
    error_out[...] = jnp.sqrt(both[0:1] / both[1:2] + 1e-06)
    for mask in range(1, n):
        error_copy(mask).wait_send()
    for store in results:
        store.wait()


def store_kernel(rate_in, state_in, error_in, rate_out, state_out, error_out, sems):
    part = rate_in.shape[0] // PIECES
    copies = [pltpu.make_async_copy(error_in, error_out, sems.at[2 * PIECES])]
    for i, (source, target) in enumerate(((rate_in, rate_out), (state_in, state_out))):
        for q in range(PIECES):
            piece = pl.ds(q * part, part)
            copies.append(
                pltpu.make_async_copy(
                    source.at[piece], target.at[piece], sems.at[i * PIECES + q]
                )
            )
    for copy in copies:
        copy.start()
    for copy in copies:
        copy.wait()


def on_device(
    log_rate,
    log_state,
    near_blocks,
    near_columns,
    far_basis,
    far_coupling,
    self_stiffness,
    plate_rate,
    direct_effect,
    evolution_effect,
    triangle_area,
):
    row_count, scenarios = log_rate.shape
    rows, near_count, size, _ = near_blocks.shape
    n = lax.axis_size("patch")
    levels, rank, _ = far_basis.shape
    total_blocks = n * rows
    first_block = lax.axis_index("patch") * rows
    local_index = jnp.arange(rows, dtype=jnp.int32)
    per_piece = rows // PIECES
    slot = (near_columns - (first_block + local_index)[:, None] + total_blocks + REACH) % total_blocks
    hit = slot[:, None, :] == jnp.arange(WIDE, dtype=jnp.int32)[None, :, None]
    none = per_piece * near_count
    place = (local_index % per_piece)[:, None, None] * near_count + jnp.arange(
        near_count, dtype=jnp.int32
    )
    index = none + jnp.sum(jnp.where(hit, place - none, 0), axis=2)

    def by_block(vector):
        return vector.reshape(rows, size)

    padded_vectors = -(-5 * rows // 128) * 128
    far_rows = levels * rank
    ext_rows = (rows + 2 * REACH) * size
    f32, bf16 = jnp.float32, jnp.bfloat16
    dma = pltpu.SemaphoreType.DMA
    anywhere = pl.BlockSpec(memory_space=pl.ANY)
    in_hbm = pl.BlockSpec(memory_space=pltpu.HBM)
    new_rate, new_state, error = pl.pallas_call(
        functools.partial(kernel, n, rows, size, levels, rank),
        out_shape=(
            pltpu.VMEM((row_count, scenarios), f32),
            pltpu.VMEM((row_count, scenarios), f32),
            pltpu.VMEM((1, scenarios), f32),
        ),
        in_specs=[pl.BlockSpec(memory_space=pltpu.SMEM)] + [in_hbm] * 10,
        out_specs=(anywhere, anywhere, pl.BlockSpec(memory_space=pltpu.VMEM)),
        scratch_shapes=[
            pltpu.VMEM((per_piece * near_count + 1, size, size), bf16) for _ in range(PIECES)
        ]
        + [
            pltpu.VMEM((row_count, scenarios), f32),
            pltpu.VMEM((row_count, scenarios), f32),
            pltpu.VMEM((far_rows, row_count), bf16),
            pltpu.VMEM((far_rows, row_count), bf16),
            pltpu.VMEM((row_count, far_rows), bf16),
            pltpu.VMEM((padded_vectors, size), f32),
            pltpu.VMEM((5, row_count, scenarios), f32),
            pltpu.VMEM((row_count, scenarios), f32),
            pltpu.VMEM((row_count, scenarios), f32),
            pltpu.VMEM((row_count, scenarios), f32),
            pltpu.VMEM((row_count, scenarios), f32),
            pltpu.VMEM((2, ext_rows, scenarios), bf16),
            pltpu.VMEM((2, far_rows, scenarios), bf16),
            pltpu.VMEM((2, n - 1, rank, scenarios), bf16),
            pltpu.VMEM((8, scenarios), f32),
            pltpu.VMEM((n - 1, 8, scenarios), f32),
            pltpu.VMEM((row_count, scenarios), f32),
            pltpu.VMEM((row_count, scenarios), f32),
            dma((PIECES,)),
            dma((9,)),
            dma((PIECES,)),
            dma((2, rows)),
            dma((2, 2, 2)),
            dma((2, 2, 2)),
            dma((2, n - 1)),
            dma((2, n - 1)),
            dma((n - 1,)),
            dma((n - 1,)),
        ],
        compiler_params=pltpu.CompilerParams(
            collective_id=0, has_side_effects=True, vmem_limit_bytes=56 * 1024 * 1024
        ),
    )(
        index,
        log_rate,
        log_state,
        near_blocks.reshape(rows * near_count, size, size),
        far_basis.reshape(far_rows, row_count),
        far_coupling.reshape(far_rows, row_count),
        by_block(self_stiffness),
        by_block(plate_rate),
        by_block(direct_effect),
        by_block(evolution_effect),
        by_block(triangle_area),
    )
    outputs = [
        jax.ShapeDtypeStruct((row_count, scenarios), f32),
        jax.ShapeDtypeStruct((row_count, scenarios), f32),
        jax.ShapeDtypeStruct((1, scenarios), f32),
    ]
    new_rate, new_state, error = pl.pallas_call(
        store_kernel,
        out_shape=outputs,
        in_specs=[anywhere] * 3,
        out_specs=[in_hbm] * 3,
        scratch_shapes=[dma((2 * PIECES + 1,))],
        compiler_params=pltpu.CompilerParams(vmem_limit_bytes=16 * 1024 * 1024),
    )(new_rate, new_state, error)
    return (new_rate, new_state, error.reshape(-1))


def solution(mesh):
    in_specs = (
        P(("member", "patch"), None),
        P(("member", "patch"), None),
        P(("member", "patch"), None, None, None),
        P(("member", "patch"), None),
        P("member", None, "patch"),
        P("member", None, "patch"),
        P(("member", "patch")),
        P(("member", "patch")),
        P(("member", "patch")),
        P(("member", "patch")),
        P(("member", "patch")),
    )
    out_specs = (P(("member", "patch"), None), P(("member", "patch"), None), P("member"))
    return jax.shard_map(
        on_device, mesh=mesh, in_specs=in_specs, out_specs=out_specs, check_vma=False
    )
```

```python
import functools

import jax
import jax.numpy as jnp
from jax import lax
from jax.experimental import pallas as pl
from jax.experimental.pallas import tpu as pltpu
from jax.sharding import PartitionSpec as P

REACH = 6
WIDE = 2 * REACH + 1
PIECES = 4
HALF = REACH // 2

step_size = 0.1
damping = 0.5
error_scale = 0.01
MESH = pl.DeviceIdType.MESH


def flipped(me, mask):
    other = me
    bit = 1
    while bit <= mask:
        if mask & bit:
            other = other + bit * (1 - 2 * ((me // bit) % 2))
        bit *= 2
    return other


def kernel(
    n,
    rows,
    size,
    levels,
    rank,
    near_columns,
    log_rate,
    log_state,
    near,
    basis,
    coupling,
    stiff_in,
    plate_in,
    direct_in,
    evolve_in,
    area_in,
    rate_out,
    state_out,
    error_out,
    *scratch,
):
    near_bufs = scratch[:PIECES]
    (
        p_buf,
        s_buf,
        basis_buf,
        coupling_buf,
        coupling_t,
        vectors,
        columns,
        v_buf,
        kp_buf,
        ks_buf,
        acc,
        ext,
        far_own,
        far_pair,
        far_total,
        far_send,
        far_recv,
        err_send,
        err_recv,
        p_res,
        s_res,
        rate_sems,
        in_sems,
        near_sems,
        column_buf,
        index_buf,
        index_ref,
        index_sems,
        out_sems,
        halo_send,
        halo_recv,
        pair_send,
        pair_recv,
        f_send,
        f_recv,
        e_send,
        e_recv,
    ) = scratch[PIECES:]
    me = lax.axis_index("patch")
    right = lax.rem(me + 1, n)
    left = lax.rem(me + n - 1, n)
    per_piece = rows // PIECES
    near_count = near.shape[0] // rows

    barrier = pltpu.get_barrier_semaphore()
    for mask in range(1, n):
        pl.semaphore_signal(
            barrier, inc=1, device_id={"patch": flipped(me, mask)}, device_id_type=MESH
        )

    def span(first, count=1):
        return pl.ds(first * size, count * size)

    quarter = [pl.ds(q * (rows // PIECES) * size, (rows // PIECES) * size) for q in range(PIECES)]
    rate_loads = [
        pltpu.make_async_copy(log_rate.at[part], p_buf.at[part], rate_sems.at[q])
        for q, part in enumerate(quarter)
    ]
    loads = [
        pltpu.make_async_copy(basis, basis_buf, in_sems.at[1]),
        pltpu.make_async_copy(coupling, coupling_buf, in_sems.at[2]),
        pltpu.make_async_copy(log_state, s_buf, in_sems.at[3]),
    ]
    vector_loads = [
        pltpu.make_async_copy(source, vectors.at[pl.ds(i * rows, rows)], in_sems.at[4 + i])
        for i, source in enumerate((stiff_in, plate_in, direct_in, evolve_in, area_in))
    ]
    near_loads = [
        pltpu.make_async_copy(
            near.at[pl.ds(q * per_piece * near_count, per_piece * near_count)],
            near_bufs[q].at[pl.ds(0, per_piece * near_count)],
            near_sems.at[q],
        )
        for q in range(PIECES)
    ]
    index_load = pltpu.make_async_copy(near_columns, column_buf, index_sems.at[0])
    index_load.start()
    for load in rate_loads:
        load.start()
    loads[0].start()
    for load in vector_loads:
        load.start()
    loads[1].start()
    for load in near_loads:
        load.start()
    loads[2].start()
    used = 5 * rows
    if vectors.shape[0] > used:
        vectors[used:, :] = jnp.zeros((vectors.shape[0] - used, size), jnp.float32)
    for q in range(PIECES):
        near_bufs[q][per_piece * near_count] = jnp.zeros((size, size), jnp.bfloat16)

    def halo_copy(section, way, piece):
        if way == 0:
            first, target, peer = HALF * piece, rows + REACH + HALF * piece, left
        else:
            first = rows - HALF * (piece + 1)
            target, peer = REACH - HALF * (piece + 1), right
        return pltpu.make_async_remote_copy(
            src_ref=ext.at[section, span(REACH + first, HALF)],
            dst_ref=ext.at[section, span(target, HALF)],
            send_sem=halo_send.at[section, way, piece],
            recv_sem=halo_recv.at[section, way, piece],
            device_id={"patch": peer},
            device_id_type=MESH,
        )

    def pair_copy(section):
        return pltpu.make_async_remote_copy(
            src_ref=far_own.at[section],
            dst_ref=far_pair.at[section],
            send_sem=pair_send.at[section],
            recv_sem=pair_recv.at[section],
            device_id={"patch": flipped(me, 1)},
            device_id_type=MESH,
        )

    def far_copy(section, mask):
        level = mask.bit_length()
        return pltpu.make_async_remote_copy(
            src_ref=far_send.at[section, pl.ds((level - 1) * rank, rank)],
            dst_ref=far_recv.at[section, mask - 1],
            send_sem=f_send.at[section, mask - 1],
            recv_sem=f_recv.at[section, mask - 1],
            device_id={"patch": flipped(me, 2 * mask)},
            device_id_type=MESH,
        )

    def error_copy(mask):
        return pltpu.make_async_remote_copy(
            src_ref=err_send,
            dst_ref=err_recv.at[mask - 1],
            send_sem=e_send.at[mask - 1],
            recv_sem=e_recv.at[mask - 1],
            device_id={"patch": flipped(me, mask)},
            device_id_type=MESH,
        )

    near_waits = [True] * PIECES

    def near_block(r, offset):
        buf = near_bufs[r // per_piece]
        if 0 <= offset < WIDE:
            return buf[index_ref[r, offset]]
        return buf[per_piece * near_count]

    def column(vector, r):
        return columns[vector, span(r)]

    def project(section):
        projected = jnp.dot(
            basis_buf[...], ext[section, span(REACH, rows)], preferred_element_type=jnp.float32
        )
        far_own[section] = projected.astype(jnp.bfloat16)
        pair_copy(section).start()
        far_total[...] = projected[rank:]

    def share_pair(section):
        pair_copy(section).wait_recv()
        joined = far_total[...] + far_pair[
            section, pl.ds(rank, (levels - 1) * rank)
        ].astype(jnp.float32)
        far_send[section] = joined.astype(jnp.bfloat16)
        for mask in range(1, n // 2):
            far_copy(section, mask).start()

    def near_pairs(section, pairs, fresh):
        for j in pairs:
            users = range(max(0, 2 * j - 2 * REACH), min(rows, 2 * j + 2))
            if section == 0:
                for q in range(PIECES):
                    if near_waits[q] and q * per_piece in users:
                        near_loads[q].wait()
                        near_waits[q] = False
            lhs = jnp.concatenate(
                [
                    jnp.concatenate([near_block(r, 2 * j - r), near_block(r, 2 * j + 1 - r)], axis=1)
                    for r in users
                ],
                axis=0,
            )
            product = jnp.dot(lhs, ext[section, span(2 * j, 2)], preferred_element_type=jnp.float32)
            for i, r in enumerate(users):
                part = product[i * size : (i + 1) * size]
                if r in fresh:
                    acc[span(r)] = part
                    fresh.discard(r)
                else:
                    acc[span(r)] += part

    def sibling_sums(section):
        for mask in range(1, n // 2):
            far_copy(section, mask).wait_recv()
        parts = [far_pair[section, pl.ds(0, rank)]]
        for level in range(1, levels):
            low = 2 ** (level - 1)
            total = far_recv[section, low - 1].astype(jnp.float32)
            for mask in range(low + 1, 2 * low):
                total = total + far_recv[section, mask - 1].astype(jnp.float32)
            parts.append(total.astype(jnp.bfloat16))
        return jnp.concatenate(parts, axis=0)

    def rates(r, far, state):
        stress = acc[span(r)] + far
        velocity = v_buf[span(r)]
        state_rate = jnp.exp(-state) - velocity
        stress_rate = column(0, r) * (column(1, r) - velocity) - stress
        rate = (stress_rate - column(3, r) * state_rate) / (column(2, r) + damping * velocity)
        return rate, state_rate

    local_pairs = range(HALF, HALF + rows // 2)
    left_pairs = range(HALF)
    right_pairs = range(HALF + rows // 2, 2 * HALF + rows // 2)

    def finished_rows(section, fresh):
        coupled = None
        for way, pairs, parts in (
            (1, left_pairs, ((0, HALF), (HALF, HALF))),
            (0, right_pairs, ((rows - HALF, HALF), (rows - REACH, HALF))),
            (None, (), ((REACH, rows - 2 * REACH),)),
        ):
            if way is not None:
                for piece in range(2):
                    halo_copy(section, way, piece).wait_recv()
            near_pairs(section, pairs, fresh)
            if coupled is None:
                coupled = sibling_sums(section)
            for first, count in parts:
                far = jnp.dot(
                    coupling_t[span(first, count)], coupled, preferred_element_type=jnp.float32
                )
                for i in range(count):
                    yield first + i, far[i * size : (i + 1) * size]

    sends_after = {
        HALF - 1: [(0, 0)],
        rows - 1: [(1, 0)],
        REACH - 1: [(0, 1)],
        rows - HALF - 1: [(1, 1)],
    }

    index_load.wait()
    first_block = me * rows
    own_row = lax.broadcasted_iota(jnp.int32, (rows, near_count), 0)
    none = per_piece * near_count
    place = (own_row % per_piece) * near_count + lax.broadcasted_iota(
        jnp.int32, (rows, near_count), 1
    )
    slot = column_buf[...] - (own_row + first_block) + REACH
    slot = jnp.where(slot < 0, slot + n * rows, slot)
    slot = jnp.where(slot >= n * rows, slot - n * rows, slot)
    lane = lax.broadcasted_iota(jnp.int32, (rows, size), 1)
    index = jnp.full((rows, size), none, jnp.int32)
    for o in range(WIDE):
        found = jnp.sum(jnp.where(slot == o, place - none, 0), axis=1, keepdims=True)
        index = jnp.where(lane == o, jnp.clip(none + found, 0, none), index)
    index_buf[...] = index
    index_store = pltpu.make_async_copy(index_buf, index_ref, index_sems.at[1])
    index_store.start()

    for load in rate_loads:
        load.wait()

    def first_velocity(first, count):
        velocity = jnp.exp(p_buf[span(first, count)])
        v_buf[span(first, count)] = velocity
        ext[0, span(REACH + first, count)] = velocity.astype(jnp.bfloat16)

    first_velocity(0, REACH)
    first_velocity(rows - REACH, REACH)
    pl.semaphore_wait(barrier, n - 1)
    for piece in range(2):
        for way in range(2):
            halo_copy(0, way, piece).start()
    first_velocity(REACH, rows - 2 * REACH)
    loads[0].wait()
    project(0)

    for load in vector_loads:
        load.wait()
    turned = vectors[...].T
    for vector in range(5):
        for r in range(rows):
            j = vector * rows + r
            columns[vector, span(r)] = jnp.broadcast_to(
                turned[:, j : j + 1], (size, columns.shape[2])
            )
    loads[1].wait()
    for r in range(rows):
        coupling_t[span(r)] = coupling_buf[:, r * size : (r + 1) * size].T
    fresh = set(range(rows))
    index_store.wait()
    near_pairs(0, local_pairs[:2], fresh)
    share_pair(0)
    near_pairs(0, local_pairs[2:], fresh)
    loads[2].wait()
    for r, far in finished_rows(0, fresh):
        state = s_buf[span(r)]
        rate, state_rate = rates(r, far, state)
        kp_buf[span(r)] = rate
        ks_buf[span(r)] = state_rate
        velocity = jnp.exp(p_buf[span(r)] + step_size * rate)
        v_buf[span(r)] = velocity
        ext[1, span(REACH + r)] = velocity.astype(jnp.bfloat16)
        for way, piece in sends_after.get(r, ()):
            halo_copy(1, way, piece).start()

    project(1)
    fresh = set(range(rows))
    near_pairs(1, local_pairs[:2], fresh)
    share_pair(1)
    near_pairs(1, local_pairs[2:], fresh)
    half_step = 0.5 * step_size
    scale = half_step / error_scale
    weighted = jnp.zeros((8, v_buf.shape[1]), jnp.float32)
    results = []
    for r, far in finished_rows(1, fresh):
        state_one = ks_buf[span(r)]
        rate_one = kp_buf[span(r)]
        state = s_buf[span(r)]
        rate, state_rate = rates(r, far, state + step_size * state_one)
        p_res[span(r)] = p_buf[span(r)] + half_step * (rate_one + rate)
        s_res[span(r)] = state + half_step * (state_one + state_rate)
        for i, (source, target) in enumerate(((p_res, rate_out), (s_res, state_out))):
            store = pltpu.make_async_copy(
                source.at[span(r)], target.at[span(r)], out_sems.at[i, r]
            )
            store.start()
            results.append(store)
        rate_error = scale * (rate - rate_one)
        state_error = scale * (state_rate - state_one)
        squares = column(4, r) * (rate_error * rate_error + state_error * state_error)
        weighted = weighted + jnp.sum(squares.reshape(-1, 8, squares.shape[1]), axis=0)

    area = jnp.sum(vectors[4 * rows : 5 * rows, :])
    lanes = weighted.shape[1]
    err_send[:, :lanes] = jnp.sum(weighted, axis=0, keepdims=True)
    err_send[:, lanes:] = jnp.full((1, lanes), area, jnp.float32)
    for mask in range(1, n):
        error_copy(mask).start()
    for section in range(2):
        for piece in range(2):
            for way in range(2):
                halo_copy(section, way, piece).wait_send()
        pair_copy(section).wait_send()
        for mask in range(1, n // 2):
            far_copy(section, mask).wait_send()
    for mask in range(1, n):
        error_copy(mask).wait_recv()
    both = err_send[...]
    for mask in range(1, n):
        both = both + err_recv[mask - 1]
    error_out[...] = jnp.sqrt(both[:, :lanes] / both[:, lanes:] + 1e-06)
    for mask in range(1, n):
        error_copy(mask).wait_send()
    for store in results:
        store.wait()


def store_kernel(rate_in, state_in, error_in, rate_out, state_out, error_out, sems):
    part = rate_in.shape[0] // PIECES
    copies = [pltpu.make_async_copy(error_in, error_out, sems.at[2 * PIECES])]
    for i, (source, target) in enumerate(((rate_in, rate_out), (state_in, state_out))):
        for q in range(PIECES):
            piece = pl.ds(q * part, part)
            copies.append(
                pltpu.make_async_copy(
                    source.at[piece], target.at[piece], sems.at[i * PIECES + q]
                )
            )
    for copy in copies:
        copy.start()
    for copy in copies:
        copy.wait()


def on_device(
    log_rate,
    log_state,
    near_blocks,
    near_columns,
    far_basis,
    far_coupling,
    self_stiffness,
    plate_rate,
    direct_effect,
    evolution_effect,
    triangle_area,
):
    row_count, scenarios = log_rate.shape
    rows, near_count, size, _ = near_blocks.shape
    n = lax.axis_size("patch")
    levels, rank, _ = far_basis.shape
    per_piece = rows // PIECES

    def by_block(vector):
        return vector.reshape(rows, size)

    padded_vectors = -(-5 * rows // 128) * 128
    far_rows = levels * rank
    ext_rows = (rows + 2 * REACH) * size
    f32, bf16 = jnp.float32, jnp.bfloat16
    dma = pltpu.SemaphoreType.DMA
    anywhere = pl.BlockSpec(memory_space=pl.ANY)
    in_hbm = pl.BlockSpec(memory_space=pltpu.HBM)
    new_rate, new_state, error = pl.pallas_call(
        functools.partial(kernel, n, rows, size, levels, rank),
        out_shape=(
            pltpu.VMEM((row_count, scenarios), f32),
            pltpu.VMEM((row_count, scenarios), f32),
            pltpu.VMEM((1, scenarios), f32),
        ),
        in_specs=[in_hbm] * 11,
        out_specs=(anywhere, anywhere, pl.BlockSpec(memory_space=pltpu.VMEM)),
        scratch_shapes=[
            pltpu.VMEM((per_piece * near_count + 1, size, size), bf16) for _ in range(PIECES)
        ]
        + [
            pltpu.VMEM((row_count, scenarios), f32),
            pltpu.VMEM((row_count, scenarios), f32),
            pltpu.VMEM((far_rows, row_count), bf16),
            pltpu.VMEM((far_rows, row_count), bf16),
            pltpu.VMEM((row_count, far_rows), bf16),
            pltpu.VMEM((padded_vectors, size), f32),
            pltpu.VMEM((5, row_count, scenarios), f32),
            pltpu.VMEM((row_count, scenarios), f32),
            pltpu.VMEM((row_count, scenarios), f32),
            pltpu.VMEM((row_count, scenarios), f32),
            pltpu.VMEM((row_count, scenarios), f32),
            pltpu.VMEM((2, ext_rows, scenarios), bf16),
            pltpu.VMEM((2, far_rows, scenarios), bf16),
            pltpu.VMEM((2, far_rows, scenarios), bf16),
            pltpu.VMEM((far_rows - rank, scenarios), f32),
            pltpu.VMEM((2, far_rows - rank, scenarios), bf16),
            pltpu.VMEM((2, n // 2 - 1, rank, scenarios), bf16),
            pltpu.VMEM((1, 2 * scenarios), f32),
            pltpu.VMEM((n - 1, 1, 2 * scenarios), f32),
            pltpu.VMEM((row_count, scenarios), f32),
            pltpu.VMEM((row_count, scenarios), f32),
            dma((PIECES,)),
            dma((9,)),
            dma((PIECES,)),
            pltpu.VMEM((rows, near_count), jnp.int32),
            pltpu.VMEM((rows, size), jnp.int32),
            pltpu.SMEM((rows, size), jnp.int32),
            dma((2,)),
            dma((2, rows)),
            dma((2, 2, 2)),
            dma((2, 2, 2)),
            dma((2,)),
            dma((2,)),
            dma((2, n // 2 - 1)),
            dma((2, n // 2 - 1)),
            dma((n - 1,)),
            dma((n - 1,)),
        ],
        compiler_params=pltpu.CompilerParams(
            collective_id=0, has_side_effects=True, vmem_limit_bytes=56 * 1024 * 1024
        ),
    )(
        near_columns,
        log_rate,
        log_state,
        near_blocks.reshape(rows * near_count, size, size),
        far_basis.reshape(far_rows, row_count),
        far_coupling.reshape(far_rows, row_count),
        by_block(self_stiffness),
        by_block(plate_rate),
        by_block(direct_effect),
        by_block(evolution_effect),
        by_block(triangle_area),
    )
    outputs = [
        jax.ShapeDtypeStruct((row_count, scenarios), f32),
        jax.ShapeDtypeStruct((row_count, scenarios), f32),
        jax.ShapeDtypeStruct((1, scenarios), f32),
    ]
    new_rate, new_state, error = pl.pallas_call(
        store_kernel,
        out_shape=outputs,
        in_specs=[anywhere] * 3,
        out_specs=[in_hbm] * 3,
        scratch_shapes=[dma((2 * PIECES + 1,))],
        compiler_params=pltpu.CompilerParams(vmem_limit_bytes=16 * 1024 * 1024),
    )(new_rate, new_state, error)
    return (new_rate, new_state, error.reshape(-1))


def solution(mesh):
    in_specs = (
        P(("member", "patch"), None),
        P(("member", "patch"), None),
        P(("member", "patch"), None, None, None),
        P(("member", "patch"), None),
        P("member", None, "patch"),
        P("member", None, "patch"),
        P(("member", "patch")),
        P(("member", "patch")),
        P(("member", "patch")),
        P(("member", "patch")),
        P(("member", "patch")),
    )
    out_specs = (P(("member", "patch"), None), P(("member", "patch"), None), P("member"))
    return jax.shard_map(
        on_device, mesh=mesh, in_specs=in_specs, out_specs=out_specs, check_vma=False
    )
```
